32 devices in a mesh: groups: 2 (over x), blk: 16 (over z, y, core).
Axes of the slice: x: 2, y: 2, z: 4, core: 2. Of those that a mesh axis runs over, the one named last changes fastest.
Arguments:
- environments: bfloat16 [40960, 4096], P(('groups', 'blk')), parts along dimension 0, may hold values from -40 to 40
- targets: bfloat16 [3, 40960], P(None, ('groups', 'blk')), parts along dimension 1, may hold values from -1 to 3
- sparse_points: bfloat16 [128, 4096], P(('groups', 'blk')), parts along dimension 0, may hold values from -0.09375 to 0.09375
- block_pair: int32 [2560], P(('groups', 'blk')), parts along dimension 0, may hold values from 0 to 7
- coupling: int32 [8, 8], replicated, may hold values from 0 to 1, as said below
Outputs:
- gram: float32 [128, 64], P(('groups', 'blk')), parts along dimension 0
- projected: float32 [3, 128], P(None, ('groups', 'blk')), parts along dimension 1
The draws below stay inside these ranges and needn't reach their ends.
There are 2 independent parts, one for each index of `groups`. The reference program is written for one: setup_inputs(seed, part) draws one part's arguments, and reference() takes and returns one part's arrays. A program takes and returns all parts, laid end to end along the dimension named above; an argument that names none is the same for every part. Nothing has to cross between parts.
Inputs may be any that keep to these rules, and one draw needn't show every extreme that they name: coupling[p, p] is 1 for every p.
All inputs are finite; a program needn't handle non-finite values.
Results may differ from the reference program's by a relative error of at most 0.0003.
Values may be sent and summed in bfloat16 or wider, within the bound.
A program may use at most 64 MiB of HBM per device.

```python
import jax
import jax.numpy as jnp
from jax import lax

D = 4096
HEADS = 3
EBLK = 16
PAIRS = 8
ENV_DEV = 1280
M = 64
ENVS = 20480
FBLOCKS = 1280


def draw_environments(key, part):
    key = jax.random.fold_in(key, 11)
    first, second, third = jax.random.split(key, 3)
    rows = ENVS
    blocks = rows // EBLK
    noise = jax.random.normal(first, (rows, D), jnp.float32)
    offset = 0.6 * jax.random.normal(second, (blocks, 1, D), jnp.float32)
    values = (noise.reshape(blocks, EBLK, D) + offset).reshape(rows, D)
    spread = jnp.exp(jax.random.uniform(third, (rows, 1), jnp.float32, jnp.log(0.7), jnp.log(1.6)))
    rising = 1.0 + 0.5 * jnp.arange(rows, dtype=jnp.float32)[:, None] / rows
    return (values * spread * rising).astype(jnp.bfloat16)


def draw_coupling(key, part):
    key = jax.random.fold_in(key, 23)
    links = jax.random.randint(key, (PAIRS, PAIRS), 0, 2)
    return jnp.maximum(links, jnp.eye(PAIRS, dtype=jnp.int32))


def place_ends(drawn, rng, smallest, high):
    index_at = [jax.random.randint(jax.random.fold_in(rng, axis), (), 0, length) for axis, length in enumerate(drawn.shape)]
    widest = drawn.shape.index(max(drawn.shape))
    next_to = index_at[:widest] + [(index_at[widest] + 1) % drawn.shape[widest]] + index_at[widest + 1:]
    return drawn.at[tuple(index_at)].set(smallest).at[tuple(next_to)].set(high)


def level_of(rng, extent, shards, low, high):
    loudness = 1.0
    for position, parts in shards:
        steps = jax.random.uniform(jax.random.fold_in(jax.random.fold_in(rng, 6), position), (parts,), jnp.float32, low / len(shards), high / len(shards))
        loudness = loudness * jnp.repeat(jnp.exp(steps), extent[position] // parts).reshape((-1,) + (1,) * (len(extent) - 1 - position))
    return loudness


def bell_draw(rng, shape, width, most, shards=(), kind=jnp.bfloat16):
    entries = width * jax.random.normal(rng, shape, jnp.float32)
    if shards:
        entries = entries * level_of(rng, shape, shards, -0.22, 0.18)
    return jnp.clip(entries, -most, most).astype(kind)


def setup_inputs(seed: int = 0, part: int = 0) -> dict:
    keys = jax.random.split(jax.random.key(seed), 6)
    part_keys = jax.random.split(jax.random.fold_in(keys[5], part), 6)
    environments = draw_environments(jax.random.fold_in(jax.random.fold_in(keys[5], part), 71), part)
    targets = jnp.clip(-1.0 + 4.0 * jax.random.uniform(part_keys[1], (HEADS, ENVS), jnp.float32) ** level_of(part_keys[1], (HEADS, ENVS), ((1, 16),), -0.2, 0.2), -1.0, 3.0).astype(jnp.bfloat16)
    sparse_points = bell_draw(part_keys[2], (M, D), D ** -0.5, 0.09375, ((0, 16),))
    block_pair = place_ends(jax.random.randint(part_keys[3], (FBLOCKS,), 0, PAIRS), jax.random.fold_in(part_keys[3], 1), 0, PAIRS - 1).astype(jnp.int32)
    coupling = draw_coupling(jax.random.fold_in(keys[5], 71), part)
    return {"environments": environments, "targets": targets, "sparse_points": sparse_points, "block_pair": block_pair, "coupling": coupling}


def reference(environments, targets, sparse_points, block_pair, coupling):
    total = environments.shape[0]
    points = sparse_points.shape[0]
    per_pair = points // PAIRS
    count = total // ENV_DEV
    col_pair = jnp.arange(points, dtype=jnp.int32) // per_pair
    col_onehot = (col_pair[:, None] == jnp.arange(PAIRS, dtype=jnp.int32)[None, :]).astype(jnp.float32)
    col_mask = jnp.dot(coupling.astype(jnp.float32), col_onehot.T)
    envs = environments.reshape(count, ENV_DEV, D)
    heads = targets.reshape(HEADS, count, ENV_DEV).transpose(1, 0, 2)
    pairs = block_pair.reshape(count, ENV_DEV // EBLK)

    def step(carry, item):
        block_x, block_y, block_p = item
        env_pair = jnp.repeat(block_p, EBLK)
        onehot = (env_pair[:, None] == jnp.arange(PAIRS, dtype=jnp.int32)[None, :]).astype(jnp.float32)
        mask = jnp.dot(onehot, col_mask)
        dots = jnp.dot(block_x, sparse_points.T, preferred_element_type=jnp.float32)
        kernel = (mask * dots * dots).astype(jnp.bfloat16)
        gram_sum = carry[0] + lax.dot_general(kernel, kernel, (((0,), (0,)), ((), ())), preferred_element_type=jnp.float32)
        proj_sum = carry[1] + jnp.dot(block_y, kernel, preferred_element_type=jnp.float32)
        return (gram_sum, proj_sum), None

    start = (jnp.zeros((points, points), jnp.float32), jnp.zeros((HEADS, points), jnp.float32))
    (gram_sum, proj_sum), _ = lax.scan(step, start, (envs, heads, pairs))
    return gram_sum / total, proj_sum / total
```

```python
import functools

import jax
import jax.numpy as jnp
from jax import lax
from jax.experimental import pallas as pl
from jax.experimental.pallas import tpu as pltpu
from jax.sharding import PartitionSpec as P

EBLK = 16
PAIRS = 8
LANES = 128
CHUNKS = 4
MESH = pl.DeviceIdType.MESH


def grid_of(devices):
    chips = devices // 2
    inner = 1
    while (inner * 2) ** 2 <= chips and chips % (inner * 2) == 0:
        inner *= 2
    return chips // inner, inner


def kernel(
    n,
    env_hbm,
    tgt_hbm,
    pts_hbm,
    pair_hbm,
    coup_hbm,
    out_ref,
    env,
    tgt,
    pair,
    coup,
    gathered,
    acc,
    part,
    landed,
    env_sem,
    small_sem,
    own_sem,
    send_sem,
    recv_sem,
    part_send,
    part_recv,
):
    outer, inner = grid_of(n)
    group = lax.axis_index("groups")
    me = lax.axis_index("blk")
    core = me % 2
    row = (me // 2) // inner
    col = (me // 2) % inner
    rows = env_hbm.shape[0]
    width = env_hbm.shape[1] // CHUNKS
    piece = pts_hbm.shape[0] // CHUNKS
    tiles = width // LANES
    pts_dev = pts_hbm.shape[0] * LANES // env_hbm.shape[1]
    points = pts_dev * n
    per_pair = points // PAIRS
    heads = tgt_hbm.shape[0]
    blocks = rows // EBLK

    def index(r, c, k):
        return (r * inner + c) * 2 + k

    loads = [
        pltpu.make_async_copy(env_hbm.at[:, pl.ds(c * width, width)], env.at[c], env_sem.at[c])
        for c in range(CHUNKS)
    ]
    small = [
        pltpu.make_async_copy(src, dst, small_sem.at[i])
        for i, (src, dst) in enumerate(((pair_hbm, pair), (coup_hbm, coup), (tgt_hbm, tgt)))
    ]
    own = pltpu.make_async_copy(pts_hbm, gathered.at[me], own_sem)
    barrier = pltpu.get_barrier_semaphore()
    for k in range(1, n):
        pl.semaphore_signal(
            barrier, inc=1, device_id=(group, (me + k) % n), device_id_type=MESH
        )
    small[0].start()
    small[1].start()
    own.start()
    for load in loads:
        load.start()
    small[2].start()

    small[0].wait()
    small[1].wait()
    label = lax.broadcasted_iota(jnp.int32, (PAIRS, blocks), 0)
    block_onehot = (label == pair[...]).astype(jnp.bfloat16)
    first = lax.broadcasted_iota(jnp.int32, (PAIRS, points), 0) * per_pair
    point = lax.broadcasted_iota(jnp.int32, (PAIRS, points), 1)
    point_onehot = ((point >= first) & (point < first + per_pair)).astype(jnp.bfloat16)
    links = jnp.dot(
        coup[...].astype(jnp.bfloat16), point_onehot, preferred_element_type=jnp.float32
    )
    mask = lax.dot_general(
        block_onehot,
        links.astype(jnp.bfloat16),
        (((0,), (0,)), ((), ())),
        preferred_element_type=jnp.float32,
    )
    pl.semaphore_wait(barrier, n - 1)

    sent = []

    def send(source, c, target, from_own):
        here = pl.ds(c * piece, piece)
        src = pts_hbm.at[here] if from_own else gathered.at[source, here]
        copy = pltpu.make_async_remote_copy(
            src_ref=src,
            dst_ref=gathered.at[source, here],
            send_sem=send_sem.at[len(sent)],
            recv_sem=recv_sem.at[source, c],
            device_id=(group, target),
            device_id_type=MESH,
        )
        copy.start()
        sent.append(copy)

    def arrived(source, c):
        here = pl.ds(c * piece, piece)
        pltpu.make_async_remote_copy(
            src_ref=gathered.at[source, here],
            dst_ref=gathered.at[source, here],
            send_sem=send_sem.at[0],
            recv_sem=recv_sem.at[source, c],
            device_id=(group, (me + 1) % n),
            device_id_type=MESH,
        ).wait_recv()

    partner = index(row, col, 1 - core)
    for c in range(CHUNKS):
        for k in range(1, outer):
            send(me, c, index((row + k) % outer, col, core), True)
        for k in range(1, inner):
            send(me, c, index(row, (col + k) % inner, core), True)
        send(me, c, partner, True)

    def relay(c):
        for k in range(1, outer):
            source = index((row + k) % outer, col, core)
            arrived(source, c)
            for j in range(1, inner):
                send(source, c, index(row, (col + j) % inner, core), False)
            send(source, c, partner, False)
        for k in range(outer):
            for j in range(1, inner):
                source = index((row + k) % outer, (col + j) % inner, core)
                arrived(source, c)
                send(source, c, partner, False)

    def multiply(c):
        for r in range(outer):
            for j in range(inner):
                arrived(index((row + r) % outer, (col + j) % inner, 1 - core), c)
        got = gathered[:, pl.ds(c * piece, piece), :].astype(jnp.float32)
        columns = []
        for t in range(tiles):
            columns.append(
                jnp.concatenate(
                    [got[d, t * pts_dev : (t + 1) * pts_dev, :] for d in range(n)], axis=0
                )
            )
        weights = jnp.concatenate(columns, axis=1).astype(jnp.bfloat16)
        loads[c].wait()
        dots = lax.dot_general(
            env[c], weights, (((1,), (1,)), ((), ())), preferred_element_type=jnp.float32
        )
        if c == 0:
            acc[...] = dots
        elif c < CHUNKS - 1:
            acc[...] += dots
        else:
            return acc[...] + dots

    own.wait()
    relay(0)
    for c in range(1, CHUNKS):
        relay(c)
        multiply(c - 1)
    dots = multiply(CHUNKS - 1).reshape(blocks, EBLK, points)
    values = (mask[:, None, :] * dots * dots).reshape(rows, points).astype(jnp.bfloat16)
    small[2].wait()
    gram = lax.dot_general(
        values, values, (((0,), (0,)), ((), ())), preferred_element_type=jnp.float32
    )
    proj = lax.dot_general(
        values, tgt[...], (((0,), (1,)), ((), ())), preferred_element_type=jnp.float32
    )
    part[:, :, :points] = gram.reshape(n, pts_dev, points)
    part[:, :, points : points + heads] = proj.reshape(n, pts_dev, heads)
    parts = []
    for k in range(1, n):
        target = (me + k) % n
        copy = pltpu.make_async_remote_copy(
            src_ref=part.at[target],
            dst_ref=landed.at[me],
            send_sem=part_send.at[k],
            recv_sem=part_recv.at[me],
            device_id=(group, target),
            device_id_type=MESH,
        )
        copy.start()
        parts.append(copy)
    landed[me] = part[me]
    for copy in sent:
        copy.wait_send()
    for k in range(1, n):
        source = (me + k) % n
        pltpu.make_async_remote_copy(
            src_ref=part.at[source],
            dst_ref=landed.at[source],
            send_sem=part_send.at[k],
            recv_sem=part_recv.at[source],
            device_id=(group, source),
            device_id_type=MESH,
        ).wait_recv()
    out_ref[...] = jnp.sum(landed[...], axis=0) / (rows * n)
    for copy in parts:
        copy.wait_send()


def shards(n, environments, targets, sparse_points, block_pair, coupling):
    rows, depth = environments.shape
    pts_dev = sparse_points.shape[0]
    points = pts_dev * n
    heads = targets.shape[0]
    blocks = block_pair.shape[0]
    outer, inner = grid_of(n)
    across = pl.cdiv(points + heads, LANES) * LANES
    flat = (
        sparse_points.reshape(pts_dev, depth // LANES, LANES)
        .transpose(1, 0, 2)
        .reshape(pts_dev * depth // LANES, LANES)
    )
    sends = CHUNKS * (outer - 1 + inner - 1 + 1 + (outer - 1) * inner + outer * (inner - 1))
    sums = pl.pallas_call(
        functools.partial(kernel, n),
        out_shape=jax.ShapeDtypeStruct((pts_dev, across), jnp.float32),
        in_specs=[pl.BlockSpec(memory_space=pl.ANY)] * 5,
        out_specs=pl.BlockSpec(memory_space=pltpu.VMEM),
        scratch_shapes=[
            pltpu.VMEM((CHUNKS, rows, depth // CHUNKS), jnp.bfloat16),
            pltpu.VMEM((heads, rows), jnp.bfloat16),
            pltpu.VMEM((1, blocks), jnp.int32),
            pltpu.VMEM((PAIRS, PAIRS), jnp.int32),
            pltpu.VMEM((n,) + flat.shape, jnp.bfloat16),
            pltpu.VMEM((rows, points), jnp.float32),
            pltpu.VMEM((n, pts_dev, across), jnp.float32),
            pltpu.VMEM((n, pts_dev, across), jnp.float32),
            pltpu.SemaphoreType.DMA((CHUNKS,)),
            pltpu.SemaphoreType.DMA((3,)),
            pltpu.SemaphoreType.DMA,
            pltpu.SemaphoreType.DMA((sends,)),
            pltpu.SemaphoreType.DMA((n, CHUNKS)),
            pltpu.SemaphoreType.DMA((n,)),
            pltpu.SemaphoreType.DMA((n,)),
        ],
        compiler_params=pltpu.CompilerParams(
            collective_id=0, has_side_effects=True, vmem_limit_bytes=48 * 2**20
        ),
        name="normal_equations",
    )(environments, targets, flat, block_pair.reshape(1, blocks), coupling)
    return sums[:, :points], sums[:, points : points + heads].T


def solution(mesh):
    in_specs = (
        P(("groups", "blk"), None),
        P(None, ("groups", "blk")),
        P(("groups", "blk"), None),
        P(("groups", "blk")),
        P(),
    )
    out_specs = (P(("groups", "blk"), None), P(None, ("groups", "blk")))
    return jax.shard_map(
        functools.partial(shards, mesh.shape["blk"]),
        mesh=mesh,
        in_specs=in_specs,
        out_specs=out_specs,
        check_vma=False,
    )
```

```python
import functools

import jax
import jax.numpy as jnp
from jax import lax
from jax.experimental import pallas as pl
from jax.experimental.pallas import tpu as pltpu
from jax.sharding import PartitionSpec as P

EBLK = 16
PAIRS = 8
LANES = 128
LEGS = 1
CHUNKS = LEGS
VMEM_BYTES = 63 * 2**20
MESH = pl.DeviceIdType.MESH


def grid_of(devices):
    chips = devices // 2
    inner = 1
    while (inner * 2) ** 2 <= chips and chips % (inner * 2) == 0:
        inner *= 2
    return chips // inner, inner


def kernel(
    n,
    env_hbm,
    tgt_hbm,
    pts_hbm,
    pair_hbm,
    coup_hbm,
    out_ref,
    env,
    tgt,
    pair,
    coup,
    gathered,
    acc,
    part,
    landed,
    env_sem,
    small_sem,
    own_sem,
    send_sem,
    recv_sem,
    part_send,
    part_recv,
):
    outer, inner = grid_of(n)
    group = lax.axis_index("groups")
    me = lax.axis_index("blk")
    core = lax.rem(me, 2)
    chip = lax.div(me, 2)
    row = lax.div(chip, inner)
    col = lax.rem(chip, inner)
    plane = outer * inner
    rows = env_hbm.shape[0]
    width = env_hbm.shape[1] // CHUNKS
    piece = pts_hbm.shape[0] // CHUNKS
    leg = pts_hbm.shape[0] // LEGS
    tiles = width // LANES
    pts_dev = pts_hbm.shape[0] * LANES // env_hbm.shape[1]
    points = pts_dev * n
    per_pair = points // PAIRS
    heads = tgt_hbm.shape[0]
    blocks = rows // EBLK

    def index(r, c, k):
        return (r * inner + c) * 2 + k

    def slot(r, c, k):
        return (k * inner + c) * outer + r

    def other(k):
        return lax.rem(me + k, n)

    loads = [
        pltpu.make_async_copy(env_hbm.at[:, pl.ds(c * width, width)], env.at[c], env_sem.at[c])
        for c in range(CHUNKS)
    ]
    small = [
        pltpu.make_async_copy(src, dst, small_sem.at[i])
        for i, (src, dst) in enumerate(((pair_hbm, pair), (coup_hbm, coup), (tgt_hbm, tgt)))
    ]
    own = pltpu.make_async_copy(pts_hbm, gathered.at[slot(row, col, core)], own_sem)
    barrier = pltpu.get_barrier_semaphore()
    for k in range(1, n):
        pl.semaphore_signal(
            barrier, inc=1, device_id=(group, other(k)), device_id_type=MESH
        )
    small[0].start()
    small[1].start()
    own.start()
    for load in loads:
        load.start()
    small[2].start()

    pl.semaphore_wait(barrier, n - 1)

    def copy(first, count, c, target, sem):
        block = gathered.at[pl.ds(first, count), pl.ds(c * leg, leg)]
        return pltpu.make_async_remote_copy(
            src_ref=block,
            dst_ref=block,
            send_sem=send_sem,
            recv_sem=recv_sem.at[sem, c],
            device_id=(group, target),
            device_id_type=MESH,
        )

    partner = index(row, col, 1 - core)
    mine = slot(row, col, core)
    down = [lax.rem(row + k, outer) for k in range(outer)]
    aside = [lax.rem(col + k, inner) for k in range(inner)]
    own.wait()
    for c in range(LEGS):
        for j in range(inner):
            for k in range(outer):
                if j + k:
                    copy(mine, 1, c, index(down[k], aside[j], core), mine).start()

    def relay(c):
        for j in range(inner):
            for k in range(outer):
                if j + k:
                    source = slot(down[k], aside[j], core)
                    copy(source, 1, c, me, source).wait_recv()
            copy(slot(0, aside[j], core), outer, c, partner, n + aside[j]).start()

    def settle(c):
        for j in range(inner):
            copy(slot(0, aside[j], 1 - core), outer, c, me, n + aside[j]).wait_recv()

    small[0].wait()
    small[1].wait()
    label = lax.broadcasted_iota(jnp.int32, (PAIRS, blocks), 0)
    block_onehot = (label == pair[...]).astype(jnp.bfloat16)
    first = lax.broadcasted_iota(jnp.int32, (PAIRS, points), 0) * per_pair
    point = lax.broadcasted_iota(jnp.int32, (PAIRS, points), 1)
    point_onehot = ((point >= first) & (point < first + per_pair)).astype(jnp.bfloat16)
    links = jnp.dot(
        coup[...].astype(jnp.bfloat16), point_onehot, preferred_element_type=jnp.float32
    )
    mask = lax.dot_general(
        block_onehot,
        links.astype(jnp.bfloat16),
        (((0,), (0,)), ((), ())),
        preferred_element_type=jnp.float32,
    )

    def multiply(c):
        if c == 0:
            for load in loads:
                load.wait()
        got = gathered[:, pl.ds(c * piece, piece), :].astype(jnp.float32)
        columns = []
        for t in range(tiles):
            columns.append(
                jnp.concatenate(
                    [got[slot(r, j, k), t * pts_dev : (t + 1) * pts_dev, :]
                     for r in range(outer) for j in range(inner) for k in range(2)], axis=0
                )
            )
        weights = jnp.concatenate(columns, axis=1).astype(jnp.bfloat16)
        dots = lax.dot_general(
            env[c], weights, (((1,), (1,)), ((), ())), preferred_element_type=jnp.float32
        )
        if CHUNKS == 1:
            return dots
        if c == 0:
            acc[...] = dots
        elif c < CHUNKS - 1:
            acc[...] += dots
        else:
            return acc[...] + dots

    done = 0
    for c in range(LEGS):
        relay(c)
        if c:
            settle(c - 1)
            while (done + 1) * LEGS <= c * CHUNKS:
                multiply(done)
                done += 1
    settle(LEGS - 1)
    while done < CHUNKS:
        dots = multiply(done)
        done += 1
    dots = dots.reshape(blocks, EBLK, points)
    values = (mask[:, None, :] * dots * dots).reshape(rows, points).astype(jnp.bfloat16)
    small[2].wait()
    gram = lax.dot_general(
        values, values, (((0,), (0,)), ((), ())), preferred_element_type=jnp.float32
    )
    proj = lax.dot_general(
        values, tgt[...], (((0,), (1,)), ((), ())), preferred_element_type=jnp.float32
    )
    part[:, :, :points] = gram.reshape(n, pts_dev, points)
    part[:, :, points : points + heads] = proj.reshape(n, pts_dev, heads)
    for k in range(1, n):
        pltpu.make_async_remote_copy(
            src_ref=part.at[other(k)],
            dst_ref=landed.at[me],
            send_sem=part_send,
            recv_sem=part_recv,
            device_id=(group, other(k)),
            device_id_type=MESH,
        ).start()
    landed[me] = part[me]
    others = landed.at[pl.ds(0, n - 1)]
    sums = pltpu.make_async_remote_copy(
        src_ref=others,
        dst_ref=others,
        send_sem=part_send,
        recv_sem=part_recv,
        device_id=(group, other(1)),
        device_id_type=MESH,
    )
    sums.wait_recv()
    out_ref[...] = jnp.sum(landed[...], axis=0) / (rows * n)
    sums.wait_send()
    pltpu.make_async_remote_copy(
        src_ref=gathered.at[pl.ds(0, n - 1)],
        dst_ref=gathered.at[pl.ds(0, n - 1)],
        send_sem=send_sem,
        recv_sem=recv_sem.at[0, 0],
        device_id=(group, other(1)),
        device_id_type=MESH,
    ).wait_send()


def split(sums_ref, gram_ref, proj_ref):
    points = gram_ref.shape[1]
    heads = proj_ref.shape[0]
    gram_ref[...] = sums_ref[:, :points]
    proj_ref[...] = sums_ref[:, points : points + heads].T


def shards(n, environments, targets, sparse_points, block_pair, coupling):
    rows, depth = environments.shape
    pts_dev = sparse_points.shape[0]
    points = pts_dev * n
    heads = targets.shape[0]
    blocks = block_pair.shape[0]
    outer, inner = grid_of(n)
    across = pl.cdiv(points + heads, LANES) * LANES
    flat = (
        sparse_points.reshape(pts_dev, depth // LANES, LANES)
        .transpose(1, 0, 2)
        .reshape(pts_dev * depth // LANES, LANES)
    )
    sums = pl.pallas_call(
        functools.partial(kernel, n),
        out_shape=jax.ShapeDtypeStruct((pts_dev, across), jnp.float32),
        in_specs=[pl.BlockSpec(memory_space=pltpu.HBM)] * 5,
        out_specs=pl.BlockSpec(memory_space=pltpu.VMEM),
        scratch_shapes=[
            pltpu.VMEM((CHUNKS, rows, depth // CHUNKS), jnp.bfloat16),
            pltpu.VMEM((heads, rows), jnp.bfloat16),
            pltpu.VMEM((1, blocks), jnp.int32),
            pltpu.VMEM((PAIRS, PAIRS), jnp.int32),
            pltpu.VMEM((n,) + flat.shape, jnp.bfloat16),
            pltpu.VMEM((rows, points), jnp.float32),
            pltpu.VMEM((n, pts_dev, across), jnp.float32),
            pltpu.VMEM((n, pts_dev, across), jnp.float32),
            pltpu.SemaphoreType.DMA((CHUNKS,)),
            pltpu.SemaphoreType.DMA((3,)),
            pltpu.SemaphoreType.DMA,
            pltpu.SemaphoreType.DMA,
            pltpu.SemaphoreType.DMA((n + inner, LEGS)),
            pltpu.SemaphoreType.DMA,
            pltpu.SemaphoreType.DMA,
        ],
        compiler_params=pltpu.CompilerParams(
            collective_id=0, has_side_effects=True, vmem_limit_bytes=VMEM_BYTES
        ),
        name="normal_equations",
    )(environments, targets, flat, block_pair.reshape(1, blocks), coupling)
    return pl.pallas_call(
        split,
        out_shape=(
            jax.ShapeDtypeStruct((pts_dev, points), jnp.float32),
            jax.ShapeDtypeStruct((heads, pts_dev), jnp.float32),
        ),
        in_specs=[pl.BlockSpec(memory_space=pltpu.VMEM)],
        out_specs=[pl.BlockSpec(memory_space=pltpu.VMEM)] * 2,
        name="outputs",
    )(sums)


def solution(mesh):
    in_specs = (
        P(("groups", "blk"), None),
        P(None, ("groups", "blk")),
        P(("groups", "blk"), None),
        P(("groups", "blk")),
        P(),
    )
    out_specs = (P(("groups", "blk"), None), P(None, ("groups", "blk")))
    return jax.shard_map(
        functools.partial(shards, mesh.shape["blk"]),
        mesh=mesh,
        in_specs=in_specs,
        out_specs=out_specs,
        check_vma=False,
    )
```

```python
import functools

import jax
import jax.numpy as jnp
from jax import lax
from jax.experimental import pallas as pl
from jax.experimental.pallas import tpu as pltpu
from jax.sharding import PartitionSpec as P

EBLK = 16
PAIRS = 8
LANES = 128
LEGS = 2
RELAYED = 3
CHUNKS = 1
VMEM_BYTES = 63 * 2**20
MESH = pl.DeviceIdType.MESH


def grid_of(devices):
    chips = devices // 2
    inner = 1
    while (inner * 2) ** 2 <= chips and chips % (inner * 2) == 0:
        inner *= 2
    return chips // inner, inner


def kernel(
    n,
    env_hbm,
    tgt_hbm,
    pts_hbm,
    pair_hbm,
    coup_hbm,
    out_ref,
    env,
    tgt,
    pair,
    coup,
    gathered,
    acc,
    part,
    landed,
    env_sem,
    small_sem,
    own_sem,
    send_sem,
    recv_sem,
    part_send,
    part_recv,
):
    outer, inner = grid_of(n)
    group = lax.axis_index("groups")
    me = lax.axis_index("blk")
    core = lax.rem(me, 2)
    chip = lax.div(me, 2)
    row = lax.div(chip, inner)
    col = lax.rem(chip, inner)
    plane = outer * inner
    rows = env_hbm.shape[0]
    width = env_hbm.shape[1] // CHUNKS
    piece = pts_hbm.shape[0] // CHUNKS
    leg = pts_hbm.shape[0] * RELAYED // 8
    tiles = width // LANES
    pts_dev = pts_hbm.shape[0] * LANES // env_hbm.shape[1]
    points = pts_dev * n
    per_pair = points // PAIRS
    heads = tgt_hbm.shape[0]
    blocks = rows // EBLK

    def index(r, c, k):
        return (r * inner + c) * 2 + k

    def slot(r, c, k):
        return (k * inner + c) * outer + r

    def other(k):
        return lax.rem(me + k, n)

    loads = [
        pltpu.make_async_copy(env_hbm.at[:, pl.ds(c * width, width)], env.at[c], env_sem.at[c])
        for c in range(CHUNKS)
    ]
    small = [
        pltpu.make_async_copy(src, dst, small_sem.at[i])
        for i, (src, dst) in enumerate(((pair_hbm, pair), (coup_hbm, coup), (tgt_hbm, tgt)))
    ]
    own = pltpu.make_async_copy(pts_hbm, gathered.at[slot(row, col, core)], own_sem)
    barrier = pltpu.get_barrier_semaphore()
    for k in range(1, n):
        pl.semaphore_signal(
            barrier, inc=1, device_id=(group, other(k)), device_id_type=MESH
        )
    small[0].start()
    small[1].start()
    own.start()
    for load in loads:
        load.start()
    small[2].start()

    pl.semaphore_wait(barrier, n - 1)

    def copy(first, count, c, target, sem):
        block = gathered.at[pl.ds(first, count), pl.ds(c * leg, pts_hbm.shape[0] - leg if c else leg)]
        return pltpu.make_async_remote_copy(
            src_ref=block,
            dst_ref=block,
            send_sem=send_sem,
            recv_sem=recv_sem.at[sem, c],
            device_id=(group, target),
            device_id_type=MESH,
        )

    partner = index(row, col, 1 - core)
    mine = slot(row, col, core)
    down = [row] + [outer - 1 - t - lax.div(row + t + 1, outer) for t in range(outer - 1)]
    aside = [lax.rem(col + k, inner) for k in range(inner)]
    own.wait()
    for k in range(1, outer):
        copy(mine, 1, 0, index(down[k], col, core), mine).start()
    for j in range(1, inner):
        copy(mine, 1, 0, index(row, aside[j], core), mine).start()
    for k in [*range(1, outer), 0]:
        for j in range(inner):
            if j + k:
                copy(mine, 1, 1, index(down[k], aside[j], core), mine).start()

    small[0].wait()
    small[1].wait()
    label = lax.broadcasted_iota(jnp.int32, (PAIRS, blocks), 0)
    block_onehot = (label == pair[...]).astype(jnp.bfloat16)
    first = lax.broadcasted_iota(jnp.int32, (PAIRS, points), 0) * per_pair
    point = lax.broadcasted_iota(jnp.int32, (PAIRS, points), 1)
    point_onehot = ((point >= first) & (point < first + per_pair)).astype(jnp.bfloat16)
    links = jnp.dot(
        coup[...].astype(jnp.bfloat16), point_onehot, preferred_element_type=jnp.float32
    )
    mask = lax.dot_general(
        block_onehot,
        links.astype(jnp.bfloat16),
        (((0,), (0,)), ((), ())),
        preferred_element_type=jnp.float32,
    )

    def multiply(c):
        if c == 0:
            for load in loads:
                load.wait()
        got = gathered[:, pl.ds(c * piece, piece), :].astype(jnp.float32)
        columns = []
        for t in range(tiles):
            columns.append(
                jnp.concatenate(
                    [got[slot(r, j, k), t * pts_dev : (t + 1) * pts_dev, :]
                     for r in range(outer) for j in range(inner) for k in range(2)], axis=0
                )
            )
        weights = jnp.concatenate(columns, axis=1).astype(jnp.bfloat16)
        dots = lax.dot_general(
            env[c], weights, (((1,), (1,)), ((), ())), preferred_element_type=jnp.float32
        )
        if CHUNKS == 1:
            return dots
        if c == 0:
            acc[...] = dots
        elif c < CHUNKS - 1:
            acc[...] += dots
        else:
            return acc[...] + dots

    for k in range(1, outer):
        source = slot(down[k], col, core)
        copy(source, 1, 0, me, source).wait_recv()
        for j in range(1, inner):
            copy(source, 1, 0, index(row, aside[j], core), source).start()
    for j in range(1, inner):
        for k in range(outer):
            source = slot(down[k], aside[j], core)
            copy(source, 1, 0, me, source).wait_recv()
    here, there = slot(0, 0, core), slot(0, 0, 1 - core)
    copy(here, plane, 0, partner, n).start()
    for j in range(inner):
        for k in range(outer):
            if j + k:
                source = slot(down[k], aside[j], core)
                copy(source, 1, 1, me, source).wait_recv()
    copy(here, plane, 1, partner, n).start()
    copy(there, plane, 0, me, n).wait_recv()
    copy(there, plane, 1, me, n).wait_recv()
    dots = multiply(0)
    dots = dots.reshape(blocks, EBLK, points)
    values = (mask[:, None, :] * dots * dots).reshape(rows, points).astype(jnp.bfloat16)
    small[2].wait()
    gram = lax.dot_general(
        values, values, (((0,), (0,)), ((), ())), preferred_element_type=jnp.float32
    )
    proj = lax.dot_general(
        values, tgt[...], (((0,), (1,)), ((), ())), preferred_element_type=jnp.float32
    )
    part[:, :, :points] = gram.reshape(n, pts_dev, points)
    part[:, :, points : points + heads] = proj.reshape(n, pts_dev, heads)
    for k in range(1, n):
        pltpu.make_async_remote_copy(
            src_ref=part.at[other(k)],
            dst_ref=landed.at[me],
            send_sem=part_send,
            recv_sem=part_recv,
            device_id=(group, other(k)),
            device_id_type=MESH,
        ).start()
    landed[me] = part[me]
    others = landed.at[pl.ds(0, n - 1)]
    sums = pltpu.make_async_remote_copy(
        src_ref=others,
        dst_ref=others,
        send_sem=part_send,
        recv_sem=part_recv,
        device_id=(group, other(1)),
        device_id_type=MESH,
    )
    sums.wait_recv()
    out_ref[...] = jnp.sum(landed[...], axis=0) / (rows * n)
    sums.wait_send()
    pltpu.make_async_remote_copy(
        src_ref=gathered.at[pl.ds(0, n - 1)],
        dst_ref=gathered.at[pl.ds(0, n - 1)],
        send_sem=send_sem,
        recv_sem=recv_sem.at[0, 0],
        device_id=(group, other(1)),
        device_id_type=MESH,
    ).wait_send()


def split(sums_ref, gram_ref, proj_ref):
    points = gram_ref.shape[1]
    heads = proj_ref.shape[0]
    gram_ref[...] = sums_ref[:, :points]
    proj_ref[...] = sums_ref[:, points : points + heads].T


def shards(n, environments, targets, sparse_points, block_pair, coupling):
    rows, depth = environments.shape
    pts_dev = sparse_points.shape[0]
    points = pts_dev * n
    heads = targets.shape[0]
    blocks = block_pair.shape[0]
    outer, inner = grid_of(n)
    across = pl.cdiv(points + heads, LANES) * LANES
    flat = (
        sparse_points.reshape(pts_dev, depth // LANES, LANES)
        .transpose(1, 0, 2)
        .reshape(pts_dev * depth // LANES, LANES)
    )
    sums = pl.pallas_call(
        functools.partial(kernel, n),
        out_shape=jax.ShapeDtypeStruct((pts_dev, across), jnp.float32),
        in_specs=[pl.BlockSpec(memory_space=pltpu.HBM)] * 5,
        out_specs=pl.BlockSpec(memory_space=pltpu.VMEM),
        scratch_shapes=[
            pltpu.VMEM((CHUNKS, rows, depth // CHUNKS), jnp.bfloat16),
            pltpu.VMEM((heads, rows), jnp.bfloat16),
            pltpu.VMEM((1, blocks), jnp.int32),
            pltpu.VMEM((PAIRS, PAIRS), jnp.int32),
            pltpu.VMEM((n,) + flat.shape, jnp.bfloat16),
            pltpu.VMEM((rows, points), jnp.float32),
            pltpu.VMEM((n, pts_dev, across), jnp.float32),
            pltpu.VMEM((n, pts_dev, across), jnp.float32),
            pltpu.SemaphoreType.DMA((CHUNKS,)),
            pltpu.SemaphoreType.DMA((3,)),
            pltpu.SemaphoreType.DMA,
            pltpu.SemaphoreType.DMA,
            pltpu.SemaphoreType.DMA((n + 1, LEGS)),
            pltpu.SemaphoreType.DMA,
            pltpu.SemaphoreType.DMA,
        ],
        compiler_params=pltpu.CompilerParams(
            collective_id=0, has_side_effects=True, vmem_limit_bytes=VMEM_BYTES
        ),
        name="normal_equations",
    )(environments, targets, flat, block_pair.reshape(1, blocks), coupling)
    return pl.pallas_call(
        split,
        out_shape=(
            jax.ShapeDtypeStruct((pts_dev, points), jnp.float32),
            jax.ShapeDtypeStruct((heads, pts_dev), jnp.float32),
        ),
        in_specs=[pl.BlockSpec(memory_space=pltpu.VMEM)],
        out_specs=[pl.BlockSpec(memory_space=pltpu.VMEM)] * 2,
        name="outputs",
    )(sums)


def solution(mesh):
    in_specs = (
        P(("groups", "blk"), None),
        P(None, ("groups", "blk")),
        P(("groups", "blk"), None),
        P(("groups", "blk")),
        P(),
    )
    out_specs = (P(("groups", "blk"), None), P(None, ("groups", "blk")))
    return jax.shard_map(
        functools.partial(shards, mesh.shape["blk"]),
        mesh=mesh,
        in_specs=in_specs,
        out_specs=out_specs,
        check_vma=False,
    )
```

```python
import functools

import jax
import jax.numpy as jnp
from jax import lax
from jax.experimental import pallas as pl
from jax.experimental.pallas import tpu as pltpu
from jax.sharding import PartitionSpec as P

EBLK = 16
PAIRS = 8
LANES = 128
LEGS = 2
RELAYED = 3
CHUNKS = 1
VMEM_BYTES = 63 * 2**20
MESH = pl.DeviceIdType.MESH


def grid_of(devices):
    chips = devices // 2
    inner = 1
    while (inner * 2) ** 2 <= chips and chips % (inner * 2) == 0:
        inner *= 2
    return chips // inner, inner


def kernel(
    n,
    env_hbm,
    tgt_hbm,
    pts_hbm,
    pair_hbm,
    coup_hbm,
    out_ref,
    env,
    tgt,
    pair,
    coup,
    gathered,
    acc,
    part,
    landed,
    env_sem,
    small_sem,
    own_sem,
    send_sem,
    recv_sem,
    part_send,
    part_recv,
):
    outer, inner = grid_of(n)
    group = lax.axis_index("groups")
    me = lax.axis_index("blk")
    core = lax.rem(me, 2)
    chip = lax.div(me, 2)
    row = lax.div(chip, inner)
    col = lax.rem(chip, inner)
    plane = outer * inner
    rows = env_hbm.shape[0]
    width = env_hbm.shape[1] // CHUNKS
    piece = pts_hbm.shape[0] // CHUNKS
    leg = pts_hbm.shape[0] * RELAYED // 8
    tiles = width // LANES
    pts_dev = pts_hbm.shape[0] * LANES // env_hbm.shape[1]
    points = pts_dev * n
    per_pair = points // PAIRS
    heads = tgt_hbm.shape[0]
    blocks = rows // EBLK

    def index(r, c, k):
        return (r * inner + c) * 2 + k

    def slot(r, c, k):
        return (k * inner + c) * outer + r

    def other(k):
        return lax.rem(me + k, n)

    loads = [
        pltpu.make_async_copy(env_hbm.at[:, pl.ds(c * width, width)], env.at[c], env_sem.at[c])
        for c in range(CHUNKS)
    ]
    small = [
        pltpu.make_async_copy(src, dst, small_sem.at[i])
        for i, (src, dst) in enumerate(((pair_hbm, pair), (coup_hbm, coup), (tgt_hbm, tgt)))
    ]
    own = pltpu.make_async_copy(pts_hbm, gathered.at[slot(row, col, core)], own_sem)
    barrier = pltpu.get_barrier_semaphore()
    for k in range(1, n):
        pl.semaphore_signal(
            barrier, inc=1, device_id=(group, other(k)), device_id_type=MESH
        )
    small[0].start()
    small[1].start()
    own.start()
    for load in loads:
        load.start()
    small[2].start()

    pl.semaphore_wait(barrier, n - 1)

    def copy(first, count, c, target, sem):
        block = gathered.at[pl.ds(first, count), pl.ds(c * leg, pts_hbm.shape[0] - leg if c else leg)]
        return pltpu.make_async_remote_copy(
            src_ref=block,
            dst_ref=block,
            send_sem=send_sem,
            recv_sem=recv_sem.at[sem, c],
            device_id=(group, target),
            device_id_type=MESH,
        )

    partner = index(row, col, 1 - core)
    mine = slot(row, col, core)
    down = [row] + [outer - 1 - t - lax.div(row + t + 1, outer) for t in range(outer - 1)]
    aside = [lax.rem(col + k, inner) for k in range(inner)]
    own.wait()
    for k in range(1, outer):
        copy(mine, 1, 0, index(down[k], col, core), mine).start()
    for j in range(1, inner):
        copy(mine, 1, 0, index(row, aside[j], core), mine).start()
    for k in [*range(1, outer), 0]:
        for j in reversed(range(inner)):
            if j + k:
                copy(mine, 1, 1, index(down[k], aside[j], core), mine).start()

    small[0].wait()
    small[1].wait()
    label = lax.broadcasted_iota(jnp.int32, (PAIRS, blocks), 0)
    block_onehot = (label == pair[...]).astype(jnp.bfloat16)
    first = lax.broadcasted_iota(jnp.int32, (PAIRS, points), 0) * per_pair
    point = lax.broadcasted_iota(jnp.int32, (PAIRS, points), 1)
    point_onehot = ((point >= first) & (point < first + per_pair)).astype(jnp.bfloat16)
    links = jnp.dot(
        coup[...].astype(jnp.bfloat16), point_onehot, preferred_element_type=jnp.float32
    )
    mask = lax.dot_general(
        block_onehot,
        links.astype(jnp.bfloat16),
        (((0,), (0,)), ((), ())),
        preferred_element_type=jnp.float32,
    )

    def multiply(c):
        if c == 0:
            for load in loads:
                load.wait()
        got = gathered[:, pl.ds(c * piece, piece), :].astype(jnp.float32)
        columns = []
        for t in range(tiles):
            columns.append(
                jnp.concatenate(
                    [got[slot(r, j, k), t * pts_dev : (t + 1) * pts_dev, :]
                     for r in range(outer) for j in range(inner) for k in range(2)], axis=0
                )
            )
        weights = jnp.concatenate(columns, axis=1).astype(jnp.bfloat16)
        dots = lax.dot_general(
            env[c], weights, (((1,), (1,)), ((), ())), preferred_element_type=jnp.float32
        )
        if CHUNKS == 1:
            return dots
        if c == 0:
            acc[...] = dots
        elif c < CHUNKS - 1:
            acc[...] += dots
        else:
            return acc[...] + dots

    for k in range(1, outer):
        source = slot(down[k], col, core)
        copy(source, 1, 0, me, source).wait_recv()
        for j in range(1, inner):
            copy(source, 1, 0, index(row, aside[j], core), source).start()
    for j in range(1, inner):
        for k in range(outer):
            source = slot(down[k], aside[j], core)
            copy(source, 1, 0, me, source).wait_recv()
    here, there = slot(0, 0, core), slot(0, 0, 1 - core)
    copy(here, plane, 0, partner, n).start()
    for j in range(inner):
        for k in range(outer):
            if j + k:
                source = slot(down[k], aside[j], core)
                copy(source, 1, 1, me, source).wait_recv()
    copy(here, plane, 1, partner, n).start()
    copy(there, plane, 0, me, n).wait_recv()
    copy(there, plane, 1, me, n).wait_recv()
    dots = multiply(0)
    dots = dots.reshape(blocks, EBLK, points)
    values = (mask[:, None, :] * dots * dots).reshape(rows, points).astype(jnp.bfloat16)
    small[2].wait()
    gram = lax.dot_general(
        values, values, (((0,), (0,)), ((), ())), preferred_element_type=jnp.float32
    )
    proj = lax.dot_general(
        values, tgt[...], (((0,), (1,)), ((), ())), preferred_element_type=jnp.float32
    )
    part[:, :, :points] = gram.reshape(n, pts_dev, points)
    part[:, :, points : points + heads] = proj.reshape(n, pts_dev, heads)
    for k in range(1, n):
        pltpu.make_async_remote_copy(
            src_ref=part.at[other(k)],
            dst_ref=landed.at[me],
            send_sem=part_send,
            recv_sem=part_recv,
            device_id=(group, other(k)),
            device_id_type=MESH,
        ).start()
    landed[me] = part[me]
    others = landed.at[pl.ds(0, n - 1)]
    sums = pltpu.make_async_remote_copy(
        src_ref=others,
        dst_ref=others,
        send_sem=part_send,
        recv_sem=part_recv,
        device_id=(group, other(1)),
        device_id_type=MESH,
    )
    sums.wait_recv()
    out_ref[...] = jnp.sum(landed[...], axis=0) / (rows * n)
    sums.wait_send()
    pltpu.make_async_remote_copy(
        src_ref=gathered.at[pl.ds(0, n - 1)],
        dst_ref=gathered.at[pl.ds(0, n - 1)],
        send_sem=send_sem,
        recv_sem=recv_sem.at[0, 0],
        device_id=(group, other(1)),
        device_id_type=MESH,
    ).wait_send()


def split(sums_ref, gram_ref, proj_ref):
    points = gram_ref.shape[1]
    heads = proj_ref.shape[0]
    gram_ref[...] = sums_ref[:, :points]
    proj_ref[...] = sums_ref[:, points : points + heads].T


def shards(n, environments, targets, sparse_points, block_pair, coupling):
    rows, depth = environments.shape
    pts_dev = sparse_points.shape[0]
    points = pts_dev * n
    heads = targets.shape[0]
    blocks = block_pair.shape[0]
    outer, inner = grid_of(n)
    across = pl.cdiv(points + heads, LANES) * LANES
    flat = (
        sparse_points.reshape(pts_dev, depth // LANES, LANES)
        .transpose(1, 0, 2)
        .reshape(pts_dev * depth // LANES, LANES)
    )
    sums = pl.pallas_call(
        functools.partial(kernel, n),
        out_shape=jax.ShapeDtypeStruct((pts_dev, across), jnp.float32),
        in_specs=[pl.BlockSpec(memory_space=pltpu.HBM)] * 5,
        out_specs=pl.BlockSpec(memory_space=pltpu.VMEM),
        scratch_shapes=[
            pltpu.VMEM((CHUNKS, rows, depth // CHUNKS), jnp.bfloat16),
            pltpu.VMEM((heads, rows), jnp.bfloat16),
            pltpu.VMEM((1, blocks), jnp.int32),
            pltpu.VMEM((PAIRS, PAIRS), jnp.int32),
            pltpu.VMEM((n,) + flat.shape, jnp.bfloat16),
            pltpu.VMEM((rows, points), jnp.float32),
            pltpu.VMEM((n, pts_dev, across), jnp.float32),
            pltpu.VMEM((n, pts_dev, across), jnp.float32),
            pltpu.SemaphoreType.DMA((CHUNKS,)),
            pltpu.SemaphoreType.DMA((3,)),
            pltpu.SemaphoreType.DMA,
            pltpu.SemaphoreType.DMA,
            pltpu.SemaphoreType.DMA((n + 1, LEGS)),
            pltpu.SemaphoreType.DMA,
            pltpu.SemaphoreType.DMA,
        ],
        compiler_params=pltpu.CompilerParams(
            collective_id=0, has_side_effects=True, vmem_limit_bytes=VMEM_BYTES
        ),
        name="normal_equations",
    )(environments, targets, flat, block_pair.reshape(1, blocks), coupling)
    return pl.pallas_call(
        split,
        out_shape=(
            jax.ShapeDtypeStruct((pts_dev, points), jnp.float32),
            jax.ShapeDtypeStruct((heads, pts_dev), jnp.float32),
        ),
        in_specs=[pl.BlockSpec(memory_space=pltpu.VMEM)],
        out_specs=[pl.BlockSpec(memory_space=pltpu.VMEM)] * 2,
        name="outputs",
    )(sums)


def solution(mesh):
    in_specs = (
        P(("groups", "blk"), None),
        P(None, ("groups", "blk")),
        P(("groups", "blk"), None),
        P(("groups", "blk")),
        P(),
    )
    out_specs = (P(("groups", "blk"), None), P(None, ("groups", "blk")))
    return jax.shard_map(
        functools.partial(shards, mesh.shape["blk"]),
        mesh=mesh,
        in_specs=in_specs,
        out_specs=out_specs,
        check_vma=False,
    )
```
